128 devices in a mesh: tm: 64 (over z, y, x), row: 2 (over core).
Axes of the slice: x: 4, y: 4, z: 4, core: 2. Of those that a mesh axis runs over, the one named last changes fastest.
Arguments:
- initial: float32 [1024], replicated, may hold values from -6 to 6
- dynamics: float32 [1024, 1024], replicated, may hold values from -0.009765625 to 0.009765625
- obs_rows: bfloat16 [131072, 1024], P('tm', 'row'), may hold values from -0.1875 to 0.1875
- obs_values: bfloat16 [131072], P('tm'), may hold values from -6 to 6
- obs_slab: int32 [131072, 1], P('tm'), may hold values from 0 to 127; in each aligned block of 2048 rows (0 to 2047, 2048 to 4095, ...) at most 64 rows name the same one
Outputs:
- states: float32 [128, 1024], P('tm', 'row')
The draws below stay inside these ranges and needn't reach their ends.
Inputs may be any that keep to these rules, and one draw needn't show every extreme that they name: `obs_slab`: within the rows ingested by one index of tm, no slab is named by more than 64 rows, a bound that some block reaches of them.
All inputs are finite; a program needn't handle non-finite values.
Results may differ from the reference program's by a relative error of at most 0.0003.
Values may be sent and summed in bfloat16 or wider, within the bound.
No kernel may reach another device: no remote copies, remote signals or barrier semaphores. Data moves between devices by JAX's collectives and lax.ppermute only.
A program may use at most 128 MiB of HBM per device.

```python
import math
import jax
import jax.numpy as jnp
import numpy as np
from jax import lax

S = 1024
OBS_DEV = 2048
CAP = 64
SLABS = 128
OBS = 131072


def block_scale(key, extent, pieces, least, high):
    factor_of = 1.0
    for axis_at, blocks in pieces:
        heights = jax.random.uniform(jax.random.fold_in(jax.random.fold_in(key, 6), axis_at), (blocks,), jnp.float32, least / len(pieces), high / len(pieces))
        factor_of = factor_of * jnp.repeat(jnp.exp(heights), extent[axis_at] // blocks).reshape((-1,) + (1,) * (len(extent) - 1 - axis_at))
    return factor_of


def shared_out(rng, own, number, rows, count, top, reach, lean):
    ranking = jax.random.permutation(rng, count)
    crowded, usual = load_shares(count, rows * top, reach, lean, True), load_shares(count, rows * top, reach, lean, False)
    places = jnp.arange(count)

    def named(lengths, offset_by):
        used = int((lengths > 0).sum())
        fixed = max(1, used // 4)
        passed = fixed + (places - fixed + offset_by * (used - fixed)) % max(1, count - fixed)
        return jnp.zeros((count,), jnp.int32).at[ranking[jnp.where(places < fixed, places, passed)]].set(jnp.asarray(lengths, jnp.int32))

    lengths = jnp.where(number % 4 == 0, named(crowded, number // 4), named(usual, number - number // 4 - 1))
    mixed = jax.random.permutation(jax.random.fold_in(own, 3), count)
    giver, sink = mixed[0:count // 2 * 2:2], mixed[1:count // 2 * 2:2]
    margin = jnp.minimum(lengths[giver] - 1, reach - lengths[sink]) // 2
    margin = jnp.where((giver == ranking[0]) | (sink == ranking[0]) | (lengths[sink] == 0), 0, jnp.maximum(margin, 0))
    passed = jax.random.randint(jax.random.fold_in(own, 4), (count // 2,), 0, 1 << 20) % (margin + 1)
    lengths = lengths.at[giver].add(-passed).at[sink].add(passed)
    members = jnp.searchsorted(jnp.cumsum(lengths), jnp.arange(rows * top), side="right").astype(jnp.int32)
    grid = members.reshape(top, rows).T
    grid = grid[jax.random.permutation(jax.random.fold_in(own, 1), rows)]
    offset_by = jax.random.randint(jax.random.fold_in(own, 2), (rows, 1), 0, top)
    return jnp.take_along_axis(grid, (jnp.arange(top)[None, :] + offset_by) % top, axis=1)


def load_shares(amount, total, reach, lean, full):
    portions = [(1 << 20) // math.isqrt(rank ** lean) + 1 for rank in range(1, amount + 1)]
    largest = reach if full else min(reach, max(-(-total // amount), total * portions[0] // sum(portions)))
    least = 1 if total - largest >= amount - 1 else 0
    given, spare = [largest] + [least] * (amount - 1), total - largest - least * (amount - 1)
    while spare > 0:
        free = [i for i in range(1, amount) if given[i] < largest] or [i for i in range(1, amount) if given[i] < reach]
        pool, budget = sum([portions[i] for i in free]), spare
        for i in free:
            extra = min(reach - given[i], max(1, budget * portions[i] // pool), spare)
            given[i] = given[i] + extra
            spare = spare - extra
    return np.array(given)


def centred(own_key, shape, deviation, bound, pieces=(), held_as=jnp.bfloat16):
    array = jax.random.normal(own_key, shape, jnp.float32) * deviation
    if len(pieces) > 0:
        array = block_scale(own_key, shape, pieces, -0.22, 0.18) * array
    return jnp.clip(array, min=-bound, max=bound).astype(held_as)


def setup_inputs(seed: int = 0) -> dict:
    streams_of = jax.random.split(jax.random.key(seed), 6)
    initial = centred(streams_of[0], (S,), 1.0, 6.0, (), jnp.float32)
    dynamics = centred(streams_of[1], (S, S), (400 * S) ** -0.5, 0.009765625, (), jnp.float32)
    obs_rows = centred(streams_of[2], (OBS, S), S ** -0.5, 0.1875, ((0, 64), (1, 2)))
    obs_values = centred(streams_of[3], (OBS,), 1.0, 6.0, ((0, 64),))
    obs_slab_keys = jax.random.split(jax.random.fold_in(streams_of[4], 1), OBS // OBS_DEV)
    obs_slab_turns = jax.random.permutation(jax.random.fold_in(streams_of[4], 3), OBS // OBS_DEV)
    obs_slab = jax.vmap(lambda own, number: shared_out(jax.random.fold_in(streams_of[4], 2), own, number, OBS_DEV, SLABS, 1, CAP, 2))(obs_slab_keys, obs_slab_turns).reshape((OBS, 1))
    return dict(initial=initial, dynamics=dynamics, obs_rows=obs_rows, obs_values=obs_values, obs_slab=obs_slab)


def reference(initial, dynamics, obs_rows, obs_values, obs_slab):
    evolve = jnp.eye(S, dtype=jnp.float32) + dynamics
    rows_f32 = obs_rows.astype(jnp.float32)
    values_f32 = obs_values.astype(jnp.float32)
    target = obs_slab[:, 0]

    def advance(state, slab_index):
        moved = jnp.dot(evolve, state, precision=lax.Precision.HIGHEST)
        in_slab = (target == slab_index).astype(jnp.float32)
        misfit = in_slab * (values_f32 - jnp.dot(rows_f32, moved, precision=lax.Precision.HIGHEST))
        updated = moved + 0.3 * jnp.dot(misfit, rows_f32, precision=lax.Precision.HIGHEST)
        return updated, updated

    final_state, states = lax.scan(advance, initial, jnp.arange(SLABS, dtype=jnp.int32))
    return states
```

```python
import jax
import jax.numpy as jnp
from jax import lax
from jax.experimental import pallas as pl
from jax.experimental.pallas import tpu as pltpu
from jax.sharding import PartitionSpec as P

F32 = jnp.float32
BF16 = jnp.bfloat16
I32 = jnp.int32
OBS = 2048
CAP = 64
COLS = 512
STATE = 1024
SLABS = 128
TIME_DEVS = 64
BLOCK_SLABS = 8
INFO_ROWS = 1024
GAIN = 0.3


def owner_of(position):
    return position ^ (((position >> 4) & 1) * 12)


def dispatch_kernel(target_ref, value_ref, rows_ref, send_ref, moment_ref, slot_ref):
    step = pl.program_id(0)

    @pl.when(step == 0)
    def _():
        chunk = 256
        row = lax.broadcasted_iota(I32, (chunk, chunk), 0)
        col = lax.broadcasted_iota(I32, (chunk, chunk), 1)
        before = (row < col).astype(F32).astype(BF16)
        carry = jnp.zeros((SLABS, 1), F32)
        moment = jnp.zeros((SLABS, COLS), F32)
        for index in range(OBS // chunk):
            part = pl.ds(index * chunk, chunk)
            target = target_ref[:, part]
            member = (lax.broadcasted_iota(I32, (SLABS, chunk), 0) == target).astype(F32)
            earlier = jnp.dot(member.astype(BF16), before, preferred_element_type=F32) + carry
            rank = jnp.sum(member * earlier, axis=0, keepdims=True).astype(I32)
            carry = carry + jnp.sum(member, axis=1, keepdims=True)
            owner = (target & 1) * TIME_DEVS + owner_of(target >> 1)
            slot_ref[:, part] = owner * CAP + rank
            weighted = (member * value_ref[:, part]).astype(BF16)
            moment = moment + jnp.dot(weighted, rows_ref[part, :], preferred_element_type=F32)
        moment_ref[...] = moment

    slots = BLOCK_SLABS * CAP
    here = lax.broadcasted_iota(I32, (slots, OBS), 0) + step * slots
    pick = jnp.where(here == slot_ref[...], 1.0, 0.0).astype(BF16)
    sent = jnp.dot(pick, rows_ref[...], preferred_element_type=F32).astype(BF16)
    send_ref[...] = sent.reshape(BLOCK_SLABS, CAP, COLS)


def dispatch(target, value, rows):
    whole = lambda i: (0, 0)
    return pl.pallas_call(
        dispatch_kernel,
        grid=(SLABS // BLOCK_SLABS,),
        in_specs=[
            pl.BlockSpec((1, OBS), whole),
            pl.BlockSpec((1, OBS), whole),
            pl.BlockSpec((OBS, COLS), whole),
        ],
        out_specs=[
            pl.BlockSpec((BLOCK_SLABS, CAP, COLS), lambda i: (i, 0, 0)),
            pl.BlockSpec((SLABS, COLS), whole),
        ],
        out_shape=[
            jax.ShapeDtypeStruct((SLABS, CAP, COLS), BF16),
            jax.ShapeDtypeStruct((SLABS, COLS), F32),
        ],
        scratch_shapes=[pltpu.VMEM((1, OBS), I32)],
        compiler_params=pltpu.CompilerParams(vmem_limit_bytes=48 * 2**20),
    )(target, value, rows)


def info_kernel(rows_ref, info_ref):
    step = pl.program_id(0)

    @pl.when(step == 0)
    def _():
        info_ref[...] = jnp.zeros_like(info_ref)

    left, right = rows_ref[0], rows_ref[1]

    def gram(a, b):
        return lax.dot_general(a, b, (((0,), (0,)), ((), ())), preferred_element_type=F32)

    info_ref[:COLS, :COLS] += gram(left, left)
    info_ref[:COLS, COLS:] += gram(left, right)
    info_ref[COLS:, COLS:] += gram(right, right)

    @pl.when(step == pl.num_programs(0) - 1)
    def _():
        info_ref[COLS:, :COLS] = info_ref[:COLS, COLS:].T


def information(halves):
    count = halves.shape[1]
    return pl.pallas_call(
        info_kernel,
        grid=(count // INFO_ROWS,),
        in_specs=[pl.BlockSpec((2, INFO_ROWS, COLS), lambda i: (0, i, 0))],
        out_specs=pl.BlockSpec((STATE, STATE), lambda i: (0, 0)),
        out_shape=jax.ShapeDtypeStruct((STATE, STATE), F32),
        compiler_params=pltpu.CompilerParams(vmem_limit_bytes=48 * 2**20),
    )(halves)


def apply(matrix_t, vector):
    return jnp.sum(matrix_t * vector[:, None], axis=0)


def body(initial, dynamics, obs_rows, obs_values, obs_slab):
    row_index = lax.axis_index("row")
    position = owner_of(lax.axis_index("tm"))
    second = row_index == 1
    swap = [(0, 1), (1, 0)]
    send, partial = dispatch(
        obs_slab.reshape(1, OBS), obs_values.astype(F32).reshape(1, OBS), obs_rows
    )
    moments = lax.psum(partial, "tm")
    received = lax.all_to_all(send, ("row", "tm"), split_axis=0, concat_axis=0, tiled=True)
    info = information(received.reshape(2, TIME_DEVS * CAP, COLS))
    evolve_t = jnp.eye(STATE, dtype=F32) + dynamics.T
    own_t = evolve_t - GAIN * jnp.dot(evolve_t, info, precision=lax.Precision.HIGH)
    other_t = lax.ppermute(own_t, "row", swap)
    first_t = jnp.where(second, other_t, own_t)
    last_t = jnp.where(second, own_t, other_t)
    both_t = jnp.dot(first_t, last_t, precision=lax.Precision.HIGH)

    mine = GAIN * lax.dynamic_slice(moments, (2 * position, 0), (2, COLS))
    theirs = lax.ppermute(mine, "row", swap)
    offsets = jnp.where(
        second,
        jnp.concatenate([theirs, mine], axis=1),
        jnp.concatenate([mine, theirs], axis=1),
    )
    offset = apply(last_t, offsets[0]) + offsets[1]

    ring = [(owner_of(t), owner_of((t + 1) % TIME_DEVS)) for t in range(TIME_DEVS)]
    at_start = position == 0
    after = jnp.zeros_like(initial)
    for step in range(TIME_DEVS):
        arrived = lax.ppermute(after, "tm", ring) if step else after
        before = jnp.where(at_start, initial, arrived)
        after = apply(both_t, before) + offset
    middle = apply(first_t, before) + offsets[0]
    states = jnp.stack([middle, after])
    states = jnp.where(second, states[:, COLS:], states[:, :COLS])
    home = [(owner_of(t), t) for t in range(TIME_DEVS)]
    return lax.ppermute(states, "tm", home)


def solution(mesh):
    placed = (P(), P(), P("tm", "row"), P("tm"), P("tm", None))
    return jax.shard_map(
        body, mesh=mesh, in_specs=placed, out_specs=P("tm", "row"), check_vma=False
    )
```

```python
import jax
import jax.numpy as jnp
from jax import lax
from jax.experimental import pallas as pl
from jax.experimental.pallas import tpu as pltpu
from jax.sharding import PartitionSpec as P

F32 = jnp.float32
BF16 = jnp.bfloat16
I32 = jnp.int32
OBS = 2048
CAP = 64
COLS = 512
STATE = 1024
SLABS = 128
TIME_DEVS = 64
BLOCK_SLABS = 8
INFO_ROWS = 1024
GAIN = 0.3
GROUP = 4
BLOCKS = 16
LAG = 3
CHUNK = 256
CLOSED = True


def owner_of(position):
    return position ^ (((position >> 4) & 1) * 12)


def dispatch_kernel(target_ref, value_ref, rows_ref, send_ref, moment_ref, slot_ref):
    step = pl.program_id(0)

    @pl.when(step == 0)
    def _():
        chunk = 256
        row = lax.broadcasted_iota(I32, (chunk, chunk), 0)
        col = lax.broadcasted_iota(I32, (chunk, chunk), 1)
        before = (row < col).astype(F32).astype(BF16)
        carry = jnp.zeros((SLABS, 1), F32)
        moment = jnp.zeros((SLABS, COLS), F32)
        for index in range(OBS // chunk):
            part = pl.ds(index * chunk, chunk)
            target = target_ref[:, part]
            place = owner_of(target >> 1) * 2 + (target & 1)
            member = (lax.broadcasted_iota(I32, (SLABS, chunk), 0) == place).astype(F32)
            earlier = jnp.dot(member.astype(BF16), before, preferred_element_type=F32) + carry
            rank = jnp.sum(member * earlier, axis=0, keepdims=True).astype(I32)
            carry = carry + jnp.sum(member, axis=1, keepdims=True)
            slot_ref[:, part] = place * CAP + rank
            weighted = (member * value_ref[:, part]).astype(BF16)
            moment = moment + jnp.dot(weighted, rows_ref[part, :], preferred_element_type=F32)
        moment_ref[...] = moment

    slots = BLOCK_SLABS * CAP
    here = lax.broadcasted_iota(I32, (slots, OBS), 0) + step * slots
    pick = jnp.where(here == slot_ref[...], 1.0, 0.0).astype(BF16)
    sent = jnp.dot(pick, rows_ref[...], preferred_element_type=F32).astype(BF16)
    send_ref[...] = sent.reshape(BLOCK_SLABS, CAP, COLS)


def dispatch(target, value, rows):
    whole = lambda i: (0, 0)
    return pl.pallas_call(
        dispatch_kernel,
        grid=(SLABS // BLOCK_SLABS,),
        in_specs=[
            pl.BlockSpec((1, OBS), whole),
            pl.BlockSpec((1, OBS), whole),
            pl.BlockSpec((OBS, COLS), whole),
        ],
        out_specs=[
            pl.BlockSpec((BLOCK_SLABS, CAP, COLS), lambda i: (i, 0, 0)),
            pl.BlockSpec((SLABS, COLS), whole),
        ],
        out_shape=[
            jax.ShapeDtypeStruct((SLABS, CAP, COLS), BF16),
            jax.ShapeDtypeStruct((SLABS, COLS), F32),
        ],
        scratch_shapes=[pltpu.VMEM((1, OBS), I32)],
        cost_estimate=pl.CostEstimate(
            flops=2 * SLABS * CAP * OBS * COLS, bytes_accessed=10 * 2**20, transcendentals=0
        ),
        compiler_params=pltpu.CompilerParams(vmem_limit_bytes=48 * 2**20),
    )(target, value, rows)


def split(value):
    high = value.astype(BF16)
    return high, (value - high.astype(F32)).astype(BF16)


def product(left, right_high, right_low):
    rows = left.shape[0]
    high, low = split(left)
    both = jnp.dot(jnp.concatenate([high, low]), right_high, preferred_element_type=F32)
    return both[:rows] + (both[rows:] + jnp.dot(high, right_low, preferred_element_type=F32))


def map_kernel(rows_ref, evolve_ref, map_ref, info_ref, high_ref, low_ref):
    step = pl.program_id(0)

    @pl.when(step == 0)
    def _():
        info_ref[...] = jnp.zeros_like(info_ref)

    left = rows_ref[:, 0].reshape(INFO_ROWS, COLS)
    right = rows_ref[:, 1].reshape(INFO_ROWS, COLS)

    def gram(a, b):
        return lax.dot_general(a, b, (((0,), (0,)), ((), ())), preferred_element_type=F32)

    info_ref[:COLS, :COLS] += gram(left, left)
    info_ref[:COLS, COLS:] += gram(left, right)
    info_ref[COLS:, COLS:] += gram(right, right)

    @pl.when(step == pl.num_programs(0) - 1)
    def _():
        info_ref[COLS:, :COLS] = info_ref[:COLS, COLS:].T
        high_ref[...], low_ref[...] = split(info_ref[...])
        for index in range(STATE // CHUNK):
            part = pl.ds(index * CHUNK, CHUNK)
            evolve = evolve_ref[part, :]
            map_ref[part, :] = evolve - GAIN * product(evolve, high_ref[...], low_ref[...])


def slab_map(rows, evolve_t):
    shards = INFO_ROWS // CAP
    whole = pl.BlockSpec((STATE, STATE), lambda i: (0, 0))
    return pl.pallas_call(
        map_kernel,
        grid=(TIME_DEVS // shards,),
        in_specs=[pl.BlockSpec((shards, 2, CAP, COLS), lambda i: (i, 0, 0, 0)), whole],
        out_specs=whole,
        out_shape=jax.ShapeDtypeStruct((STATE, STATE), F32),
        scratch_shapes=[
            pltpu.VMEM((STATE, STATE), F32),
            pltpu.VMEM((STATE, STATE), BF16),
            pltpu.VMEM((STATE, STATE), BF16),
        ],
        cost_estimate=pl.CostEstimate(
            flops=2 * STATE * STATE * (TIME_DEVS * CAP + 3 * STATE),
            bytes_accessed=16 * 2**20,
            transcendentals=0,
        ),
        compiler_params=pltpu.CompilerParams(vmem_limit_bytes=48 * 2**20),
    )(rows, evolve_t)


def pair_kernel(core_ref, own_ref, other_ref, offsets_ref, high_ref, low_ref, half_ref, offset_ref, h_ref, l_ref):
    def run(first_ref, last_ref, start):
        h_ref[...], l_ref[...] = split(last_ref[...])
        for index in range(0, STATE, CHUNK):
            part = pl.ds(index, CHUNK)
            made = product(first_ref[part, :], h_ref[...], l_ref[...])
            high_ref[part, :], low_ref[part, :] = split(made)
            if start <= index < start + COLS:
                half_ref[pl.ds(index - start, CHUNK), :] = made
        first = jnp.broadcast_to(offsets_ref[0:1, :], (16, STATE))
        offset_ref[...] = product(first, h_ref[...], l_ref[...])[0:1] + offsets_ref[1:2, :]

    @pl.when(core_ref[0] == 0)
    def _():
        run(own_ref, other_ref, 0)

    @pl.when(core_ref[0] == 1)
    def _():
        run(other_ref, own_ref, COLS)


VMEM = pl.BlockSpec(memory_space=pltpu.VMEM)
SMEM = pl.BlockSpec(memory_space=pltpu.SMEM)


def shape(rows, dtype):
    return jax.ShapeDtypeStruct((rows, STATE), dtype)


def pair_map(core, own_t, other_t, offsets):
    return pl.pallas_call(
        pair_kernel,
        in_specs=[SMEM, VMEM, VMEM, VMEM],
        out_specs=[VMEM] * 4,
        out_shape=[shape(STATE, BF16), shape(STATE, BF16), shape(COLS, F32), shape(1, F32)],
        scratch_shapes=[pltpu.VMEM((STATE, STATE), BF16)] * 2,
        cost_estimate=pl.CostEstimate(
            flops=6 * STATE**3, bytes_accessed=16 * 2**20, transcendentals=0
        ),
        compiler_params=pltpu.CompilerParams(vmem_limit_bytes=48 * 2**20),
    )(core, own_t, other_t, offsets)


def step_kernel(flags_ref, arrived_ref, opening_ref, offset_ref, high_ref, low_ref, out_ref):
    made = product(arrived_ref[...], high_ref[...], low_ref[...])
    out_ref[...] = jnp.where(flags_ref[0] == 1, opening_ref[...], made)

    @pl.when(flags_ref[1] == 1)
    def _():
        out_ref[0:1, :] += offset_ref[...]


def advance(flags, arrived, opening, offset, high, low):
    return pl.pallas_call(
        step_kernel,
        in_specs=[SMEM] + [VMEM] * 5,
        out_specs=VMEM,
        out_shape=jax.ShapeDtypeStruct(arrived.shape, F32),
        cost_estimate=pl.CostEstimate(
            flops=6 * arrived.shape[0] * STATE**2, bytes_accessed=4 * 2**20, transcendentals=0
        ),
        compiler_params=pltpu.CompilerParams(vmem_limit_bytes=24 * 2**20),
    )(flags, arrived, opening, offset, high, low)


def gather_kernel(core_ref, own_ref, other_ref, high_ref, low_ref):
    def run(first_ref, last_ref):
        high_ref[:COLS, :], low_ref[:COLS, :] = split(first_ref[:COLS, :])
        high_ref[COLS:, :], low_ref[COLS:, :] = split(last_ref[:COLS, :])

    @pl.when(core_ref[0] == 0)
    def _():
        run(own_ref, other_ref)

    @pl.when(core_ref[0] == 1)
    def _():
        run(other_ref, own_ref)


def gather(core, own, other):
    return pl.pallas_call(
        gather_kernel,
        in_specs=[SMEM, VMEM, VMEM],
        out_specs=[VMEM] * 2,
        out_shape=[shape(STATE, BF16), shape(STATE, BF16)],
        compiler_params=pltpu.CompilerParams(vmem_limit_bytes=24 * 2**20),
    )(core, own, other)


def hop_kernel(mine_ref, arrived_ref, held_ref, high_ref, low_ref, offset_ref, entry_ref, after_ref):
    entry = jnp.where(mine_ref[0] == 1, arrived_ref[...], held_ref[...])
    entry_ref[...] = entry
    moved = product(jnp.broadcast_to(entry, (16, STATE)), high_ref[...], low_ref[...])
    after_ref[...] = moved[0:1] + offset_ref[...]


def hop(mine, arrived, held, high, low, offset):
    return pl.pallas_call(
        hop_kernel,
        in_specs=[SMEM] + [VMEM] * 5,
        out_specs=[VMEM] * 2,
        out_shape=[shape(1, F32), shape(1, F32)],
        cost_estimate=pl.CostEstimate(
            flops=96 * STATE**2, bytes_accessed=4 * 2**20, transcendentals=0
        ),
        compiler_params=pltpu.CompilerParams(vmem_limit_bytes=24 * 2**20),
    )(mine.astype(I32).reshape(1), arrived, held, high, low, offset)


def apply(matrix_t, vector):
    return jnp.sum(matrix_t * vector[:, None], axis=0)


def along_line(value, steps, closed=True):
    pairs = [
        (i, i // GROUP * GROUP + (i + steps) % GROUP)
        for i in range(TIME_DEVS)
        if closed or i % GROUP + steps < GROUP
    ]
    return lax.ppermute(value, "tm", pairs)


def share_over(value, stride):
    place = lax.axis_index("tm") // stride % 4
    parts = value.reshape(4, -1, *value.shape[1:])
    total = lax.dynamic_index_in_dim(parts, place, keepdims=False)
    for steps in (1, 2, 3):
        pairs = [
            (i, i // (4 * stride) * (4 * stride) + (i + steps * stride) % (4 * stride))
            for i in range(TIME_DEVS)
        ]
        sent = lax.dynamic_index_in_dim(parts, (place + steps) % 4, keepdims=False)
        total = total + lax.ppermute(sent, "tm", pairs)
    return total


def body(initial, dynamics, obs_rows, obs_values, obs_slab):
    position = owner_of(lax.axis_index("tm"))
    second = lax.axis_index("row") == 1
    swap = [(0, 1), (1, 0)]
    send, partial = dispatch(
        obs_slab.reshape(1, OBS), obs_values.astype(F32).reshape(1, OBS), obs_rows
    )
    received = lax.all_to_all(send, ("tm", "row"), split_axis=0, concat_axis=0, tiled=True)
    evolve_t = jnp.eye(STATE, dtype=F32) + dynamics.T
    moment = share_over(partial.reshape(TIME_DEVS, 2, COLS), 16)
    received, moment, evolve_t = lax.optimization_barrier((received, moment, evolve_t))
    own_t = slab_map(received.reshape(TIME_DEVS, 2, CAP, COLS), evolve_t)
    moment = share_over(moment, 4)
    own_t, moment = lax.optimization_barrier((own_t, moment))
    other_t = lax.ppermute(own_t, "row", swap)
    mine = GAIN * share_over(moment, 1)[0]
    theirs = lax.ppermute(mine, "row", swap)
    offsets = jnp.where(
        second,
        jnp.concatenate([theirs, mine], axis=1),
        jnp.concatenate([mine, theirs], axis=1),
    )
    core = lax.axis_index("row").astype(I32).reshape(1)
    high, low, own_half, offset = pair_map(core, own_t, other_t, offsets)
    first_half_t = jnp.where(second, other_t[:, COLS:], own_t[:, :COLS])

    turn = position % GROUP
    leads = turn == 0
    width = COLS // BLOCKS
    opening = [own_half[index * width :][:width] for index in range(BLOCKS)]
    opening.append(jnp.pad(offset, ((0, width - 1), (0, 0))))
    made = []
    for step in range(BLOCKS + 1 + LAG * (GROUP - 1)):
        block = opening[min(step, BLOCKS)]
        if step >= LAG:
            arrived = along_line(made[step - LAG], 1, CLOSED)
            adds = (step - LAG * turn == BLOCKS) & ~leads
            flags = jnp.stack([leads, adds]).astype(I32)
            block = advance(flags, arrived, block, offset, high, low)
        made.append(block)
    prefix_t = lax.dynamic_slice(
        jnp.concatenate(made), (turn * (LAG * width), 0), (COLS + width, STATE)
    )
    shift = prefix_t[COLS : COLS + 1]
    high, low = gather(core, prefix_t, lax.ppermute(prefix_t[:COLS], "row", swap))

    entry = initial.reshape(1, STATE)
    entry, after = hop(leads, entry, entry, high, low, shift)
    later = position >= GROUP
    next_line = [(owner_of(t), owner_of((t + GROUP) % TIME_DEVS)) for t in range(TIME_DEVS)]
    for _ in range(TIME_DEVS // GROUP - 1):
        arrived = lax.ppermute(after, "tm", next_line)
        entry, after = hop(later, arrived, entry, high, low, shift)
    held = entry
    for steps in range(1, GROUP):
        entry = jnp.where(turn == steps - 1, along_line(held, steps), entry)
    entry, after = hop(leads, entry, entry, high, low, shift)
    before = jnp.where(leads, entry, along_line(after, 1))[0]
    middle = apply(first_half_t, before) + mine[0]
    after = jnp.where(second, after[0, COLS:], after[0, :COLS])
    states = jnp.stack([middle, after])
    return lax.ppermute(states, "tm", [(owner_of(t), t) for t in range(TIME_DEVS)])


def solution(mesh):
    placed = (P(), P(), P("tm", "row"), P("tm"), P("tm", None))
    return jax.shard_map(
        body, mesh=mesh, in_specs=placed, out_specs=P("tm", "row"), check_vma=False
    )
```

```python
import functools

import jax
import jax.numpy as jnp
from jax import lax
from jax.experimental import pallas as pl
from jax.experimental.pallas import tpu as pltpu
from jax.sharding import PartitionSpec as P

F32 = jnp.float32
BF16 = jnp.bfloat16
I32 = jnp.int32
OBS = 2048
CAP = 64
COLS = 512
STATE = 1024
SLABS = 128
TIME_DEVS = 64
BLOCK_SLABS = 8
INFO_ROWS = 1024
GAIN = 0.3
GROUP = 4
BLOCKS = 16
LAG = 3
CHUNK = 256
CLOSED = True


def owner_of(position):
    return position ^ (((position >> 4) & 1) * 12)


def dispatch_kernel(target_ref, value_ref, rows_ref, send_ref, moment_ref, slot_ref):
    step = pl.program_id(0)

    @pl.when(step == 0)
    def _():
        chunk = 256
        row = lax.broadcasted_iota(I32, (chunk, chunk), 0)
        col = lax.broadcasted_iota(I32, (chunk, chunk), 1)
        before = (row < col).astype(F32).astype(BF16)
        carry = jnp.zeros((SLABS, 1), F32)
        moment = jnp.zeros((SLABS, COLS), F32)
        for index in range(OBS // chunk):
            part = pl.ds(index * chunk, chunk)
            target = target_ref[:, part]
            place = owner_of(target >> 1) * 2 + (target & 1)
            member = (lax.broadcasted_iota(I32, (SLABS, chunk), 0) == place).astype(F32)
            earlier = jnp.dot(member.astype(BF16), before, preferred_element_type=F32) + carry
            rank = jnp.sum(member * earlier, axis=0, keepdims=True).astype(I32)
            carry = carry + jnp.sum(member, axis=1, keepdims=True)
            slot_ref[:, part] = place * CAP + rank
            weighted = (member * value_ref[:, part]).astype(BF16)
            moment = moment + jnp.dot(weighted, rows_ref[part, :], preferred_element_type=F32)
        moment_ref[...] = moment

    slots = BLOCK_SLABS * CAP
    here = lax.broadcasted_iota(I32, (slots, OBS), 0) + step * slots
    pick = jnp.where(here == slot_ref[...], 1.0, 0.0).astype(BF16)
    sent = jnp.dot(pick, rows_ref[...], preferred_element_type=F32).astype(BF16)
    send_ref[...] = sent.reshape(BLOCK_SLABS, CAP, COLS)


def dispatch(target, value, rows):
    whole = lambda i: (0, 0)
    return pl.pallas_call(
        dispatch_kernel,
        grid=(SLABS // BLOCK_SLABS,),
        in_specs=[
            pl.BlockSpec((1, OBS), whole),
            pl.BlockSpec((1, OBS), whole),
            pl.BlockSpec((OBS, COLS), whole),
        ],
        out_specs=[
            pl.BlockSpec((BLOCK_SLABS, CAP, COLS), lambda i: (i, 0, 0)),
            pl.BlockSpec((SLABS, COLS), whole),
        ],
        out_shape=[
            jax.ShapeDtypeStruct((SLABS, CAP, COLS), BF16),
            jax.ShapeDtypeStruct((SLABS, COLS), F32),
        ],
        scratch_shapes=[pltpu.VMEM((1, OBS), I32)],
        cost_estimate=pl.CostEstimate(
            flops=2 * SLABS * CAP * OBS * COLS, bytes_accessed=10 * 2**20, transcendentals=0
        ),
        compiler_params=pltpu.CompilerParams(vmem_limit_bytes=48 * 2**20),
    )(target, value, rows)


def split(value):
    high = value.astype(BF16)
    return high, (value - high.astype(F32)).astype(BF16)


def product(left, right_high, right_low):
    rows = left.shape[0]
    high, low = split(left)
    both = jnp.dot(jnp.concatenate([high, low]), right_high, preferred_element_type=F32)
    return both[:rows] + (both[rows:] + jnp.dot(high, right_low, preferred_element_type=F32))


def map_kernel(rows_ref, evolve_ref, map_ref, info_ref, high_ref, low_ref):
    step = pl.program_id(0)

    @pl.when(step == 0)
    def _():
        info_ref[...] = jnp.zeros_like(info_ref)

    left = rows_ref[:, 0].reshape(INFO_ROWS, COLS)
    right = rows_ref[:, 1].reshape(INFO_ROWS, COLS)

    def gram(a, b):
        return lax.dot_general(a, b, (((0,), (0,)), ((), ())), preferred_element_type=F32)

    info_ref[:COLS, :COLS] += gram(left, left)
    info_ref[:COLS, COLS:] += gram(left, right)
    info_ref[COLS:, COLS:] += gram(right, right)

    @pl.when(step == pl.num_programs(0) - 1)
    def _():
        info_ref[COLS:, :COLS] = info_ref[:COLS, COLS:].T
        high_ref[...], low_ref[...] = split(info_ref[...])
        for index in range(STATE // CHUNK):
            part = pl.ds(index * CHUNK, CHUNK)
            evolve = evolve_ref[part, :]
            map_ref[part, :] = evolve - GAIN * product(evolve, high_ref[...], low_ref[...])


def slab_map(rows, evolve_t):
    shards = INFO_ROWS // CAP
    whole = pl.BlockSpec((STATE, STATE), lambda i: (0, 0))
    return pl.pallas_call(
        map_kernel,
        grid=(TIME_DEVS // shards,),
        in_specs=[pl.BlockSpec((shards, 2, CAP, COLS), lambda i: (i, 0, 0, 0)), whole],
        out_specs=whole,
        out_shape=jax.ShapeDtypeStruct((STATE, STATE), F32),
        scratch_shapes=[
            pltpu.VMEM((STATE, STATE), F32),
            pltpu.VMEM((STATE, STATE), BF16),
            pltpu.VMEM((STATE, STATE), BF16),
        ],
        cost_estimate=pl.CostEstimate(
            flops=2 * STATE * STATE * (TIME_DEVS * CAP + 3 * STATE),
            bytes_accessed=16 * 2**20,
            transcendentals=0,
        ),
        compiler_params=pltpu.CompilerParams(vmem_limit_bytes=48 * 2**20),
    )(rows, evolve_t)


def pair_kernel(core_ref, own_ref, other_ref, offsets_ref, high_ref, low_ref, half_ref, offset_ref, first_half_ref, h_ref, l_ref):
    def run(first_ref, last_ref, start):
        h_ref[...], l_ref[...] = split(last_ref[...])
        for index in range(0, STATE, CHUNK):
            part = pl.ds(index, CHUNK)
            made = product(first_ref[part, :], h_ref[...], l_ref[...])
            high_ref[part, :], low_ref[part, :] = split(made)
            if start <= index < start + COLS:
                half_ref[pl.ds(index - start, CHUNK), :] = made
        first_half_ref[...] = first_ref[:, start : start + COLS]
        first = jnp.broadcast_to(offsets_ref[0:1, :], (16, STATE))
        offset_ref[...] = product(first, h_ref[...], l_ref[...])[0:1] + offsets_ref[1:2, :]

    @pl.when(core_ref[0] == 0)
    def _():
        run(own_ref, other_ref, 0)

    @pl.when(core_ref[0] == 1)
    def _():
        run(other_ref, own_ref, COLS)


VMEM = pl.BlockSpec(memory_space=pltpu.VMEM)
SMEM = pl.BlockSpec(memory_space=pltpu.SMEM)


def shape(rows, dtype):
    return jax.ShapeDtypeStruct((rows, STATE), dtype)


def pair_map(core, own_t, other_t, offsets):
    return pl.pallas_call(
        pair_kernel,
        in_specs=[SMEM, VMEM, VMEM, VMEM],
        out_specs=[VMEM] * 5,
        out_shape=[
            shape(STATE, BF16),
            shape(STATE, BF16),
            shape(COLS, F32),
            shape(1, F32),
            jax.ShapeDtypeStruct((STATE, COLS), F32),
        ],
        scratch_shapes=[pltpu.VMEM((STATE, STATE), BF16)] * 2,
        cost_estimate=pl.CostEstimate(
            flops=6 * STATE**3, bytes_accessed=16 * 2**20, transcendentals=0
        ),
        compiler_params=pltpu.CompilerParams(vmem_limit_bytes=48 * 2**20),
    )(core, own_t, other_t, offsets)


def step_kernel(step, turn_ref, arrived_ref, opening_ref, offset_ref, high_ref, low_ref, out_ref):
    turn = turn_ref[0]
    made = product(arrived_ref[...], high_ref[...], low_ref[...])
    out_ref[...] = jnp.where(turn == 0, opening_ref[...], made)

    @pl.when((turn > 0) & (step - LAG * turn == BLOCKS))
    def _():
        out_ref[0:1, :] += offset_ref[...]


def advance(step, turn, arrived, opening, offset, high, low):
    return pl.pallas_call(
        functools.partial(step_kernel, step),
        in_specs=[SMEM] + [VMEM] * 5,
        out_specs=VMEM,
        out_shape=jax.ShapeDtypeStruct(arrived.shape, F32),
        cost_estimate=pl.CostEstimate(
            flops=6 * arrived.shape[0] * STATE**2, bytes_accessed=4 * 2**20, transcendentals=0
        ),
        compiler_params=pltpu.CompilerParams(vmem_limit_bytes=24 * 2**20),
    )(turn, arrived, opening, offset, high, low)


def select_kernel(turn_ref, *refs):
    made_refs, (parts_ref, shift_ref) = refs[:-2], refs[-2:]
    width = COLS // BLOCKS
    for turn in range(GROUP):

        @pl.when(turn_ref[0] == turn)
        def _(mine=made_refs[LAG * turn :]):
            for index in range(BLOCKS):
                high, low = split(mine[index][...])
                parts_ref[pl.ds(index * width, width), :] = high
                parts_ref[pl.ds(COLS + index * width, width), :] = low
            shift_ref[...] = mine[BLOCKS][0:1, :]


def select(turn, made):
    return pl.pallas_call(
        select_kernel,
        in_specs=[SMEM] + [VMEM] * len(made),
        out_specs=[VMEM] * 2,
        out_shape=[shape(STATE, BF16), shape(1, F32)],
        compiler_params=pltpu.CompilerParams(vmem_limit_bytes=24 * 2**20),
    )(turn, *made)


def gather_kernel(core_ref, own_ref, other_ref, high_ref, low_ref):
    def run(first_ref, last_ref):
        high_ref[:COLS, :] = first_ref[:COLS, :]
        high_ref[COLS:, :] = last_ref[:COLS, :]
        low_ref[:COLS, :] = first_ref[COLS:, :]
        low_ref[COLS:, :] = last_ref[COLS:, :]

    @pl.when(core_ref[0] == 0)
    def _():
        run(own_ref, other_ref)

    @pl.when(core_ref[0] == 1)
    def _():
        run(other_ref, own_ref)


def gather(core, own, other):
    return pl.pallas_call(
        gather_kernel,
        in_specs=[SMEM, VMEM, VMEM],
        out_specs=[VMEM] * 2,
        out_shape=[shape(STATE, BF16), shape(STATE, BF16)],
        compiler_params=pltpu.CompilerParams(vmem_limit_bytes=24 * 2**20),
    )(core, own, other)


def hop_kernel(mine_ref, arrived_ref, held_ref, high_ref, low_ref, offset_ref, entry_ref, after_ref):
    entry = jnp.where(mine_ref[0] == 1, arrived_ref[...], held_ref[...])
    entry_ref[...] = entry
    moved = product(jnp.broadcast_to(entry, (16, STATE)), high_ref[...], low_ref[...])
    after_ref[...] = moved[0:1] + offset_ref[...]


def hop(mine, arrived, held, high, low, offset):
    return pl.pallas_call(
        hop_kernel,
        in_specs=[SMEM] + [VMEM] * 5,
        out_specs=[VMEM] * 2,
        out_shape=[shape(1, F32), shape(1, F32)],
        cost_estimate=pl.CostEstimate(
            flops=96 * STATE**2, bytes_accessed=4 * 2**20, transcendentals=0
        ),
        compiler_params=pltpu.CompilerParams(vmem_limit_bytes=24 * 2**20),
    )(mine.astype(I32).reshape(1), arrived, held, high, low, offset)


def apply(matrix_t, vector):
    return jnp.sum(matrix_t * vector[:, None], axis=0)


def along_line(value, steps, closed=True):
    pairs = [
        (i, i // GROUP * GROUP + (i + steps) % GROUP)
        for i in range(TIME_DEVS)
        if closed or i % GROUP + steps < GROUP
    ]
    return lax.ppermute(value, "tm", pairs)


def share_over(value, stride):
    place = lax.axis_index("tm") // stride % 4
    parts = value.reshape(4, -1, *value.shape[1:])
    total = lax.dynamic_index_in_dim(parts, place, keepdims=False)
    for steps in (1, 2, 3):
        pairs = [
            (i, i // (4 * stride) * (4 * stride) + (i + steps * stride) % (4 * stride))
            for i in range(TIME_DEVS)
        ]
        sent = lax.dynamic_index_in_dim(parts, (place + steps) % 4, keepdims=False)
        total = total + lax.ppermute(sent, "tm", pairs)
    return total


def body(initial, dynamics, obs_rows, obs_values, obs_slab):
    position = owner_of(lax.axis_index("tm"))
    second = lax.axis_index("row") == 1
    swap = [(0, 1), (1, 0)]
    send, partial = dispatch(
        obs_slab.reshape(1, OBS), obs_values.astype(F32).reshape(1, OBS), obs_rows
    )
    received = lax.all_to_all(send, ("tm", "row"), split_axis=0, concat_axis=0, tiled=True)
    evolve_t = jnp.eye(STATE, dtype=F32) + dynamics.T
    moment = share_over(partial.reshape(TIME_DEVS, 2, COLS), 16)
    received, moment, evolve_t = lax.optimization_barrier((received, moment, evolve_t))
    own_t = slab_map(received.reshape(TIME_DEVS, 2, CAP, COLS), evolve_t)
    planes = [list(range(start, start + 16)) for start in range(0, TIME_DEVS, 16)]
    moment = lax.all_to_all(
        moment.reshape(16, 2 * COLS), "tm", 0, 0, tiled=True, axis_index_groups=planes
    )
    own_t, moment = lax.optimization_barrier((own_t, moment))
    other_t = lax.ppermute(own_t, "row", swap)
    mine = GAIN * jnp.sum(moment, axis=0).reshape(2, COLS)
    theirs = lax.ppermute(mine, "row", swap)
    offsets = jnp.where(
        second,
        jnp.concatenate([theirs, mine], axis=1),
        jnp.concatenate([mine, theirs], axis=1),
    )
    core = lax.axis_index("row").astype(I32).reshape(1)
    high, low, own_half, offset, first_half_t = pair_map(core, own_t, other_t, offsets)

    turn = position % GROUP
    leads = turn == 0
    turn_scalar = turn.astype(I32).reshape(1)
    width = COLS // BLOCKS
    opening = [own_half[index * width :][:width] for index in range(BLOCKS)]
    opening.append(jnp.pad(offset, ((0, width - 1), (0, 0))))
    made = []
    for step in range(BLOCKS + 1 + LAG * (GROUP - 1)):
        block = opening[min(step, BLOCKS)]
        if step >= LAG:
            arrived = along_line(made[step - LAG], 1, CLOSED)
            block = advance(step, turn_scalar, arrived, block, offset, high, low)
        made.append(block)
    own, shift = select(turn_scalar, made)
    high, low = gather(core, own, lax.ppermute(own, "row", swap))

    def whole_prefix(takes, arrived, held):
        return hop(takes, arrived, held, high, low, shift)

    entry = initial.reshape(1, STATE)
    entry, after = whole_prefix(leads, entry, entry)
    later = position >= GROUP
    next_line = [(owner_of(t), owner_of((t + GROUP) % TIME_DEVS)) for t in range(TIME_DEVS)]
    for _ in range(TIME_DEVS // GROUP - 1):
        arrived = lax.ppermute(after, "tm", next_line)
        entry, after = whole_prefix(later, arrived, entry)
    held = entry
    for steps in range(1, GROUP):
        entry = jnp.where(turn == steps - 1, along_line(held, steps), entry)
    entry, after = whole_prefix(leads, entry, entry)
    before = jnp.where(leads, entry, along_line(after, 1))[0]
    middle = apply(first_half_t, before) + mine[0]
    after = jnp.where(second, after[0, COLS:], after[0, :COLS])
    states = jnp.stack([middle, after])
    return lax.ppermute(states, "tm", [(owner_of(t), t) for t in range(TIME_DEVS)])


def solution(mesh):
    placed = (P(), P(), P("tm", "row"), P("tm"), P("tm", None))
    return jax.shard_map(
        body, mesh=mesh, in_specs=placed, out_specs=P("tm", "row"), check_vma=False
    )
```

```python
import functools

import jax
import jax.numpy as jnp
from jax import lax
from jax.experimental import pallas as pl
from jax.experimental.pallas import tpu as pltpu
from jax.sharding import PartitionSpec as P

F32 = jnp.float32
BF16 = jnp.bfloat16
I32 = jnp.int32
OBS = 2048
CAP = 64
COLS = 512
STATE = 1024
SLABS = 128
TIME_DEVS = 64
BLOCK_SLABS = 8
INFO_ROWS = 1024
GAIN = 0.3
GROUP = 4
BLOCKS = 16
LAG = 3
CHUNK = 256
CLOSED = True


def owner_of(position):
    return position ^ (((position >> 4) & 1) * 12)


def dispatch_kernel(target_ref, value_ref, rows_ref, send_ref, moment_ref, slot_ref):
    step = pl.program_id(0)

    @pl.when(step == 0)
    def _():
        chunk = 256
        row = lax.broadcasted_iota(I32, (chunk, chunk), 0)
        col = lax.broadcasted_iota(I32, (chunk, chunk), 1)
        before = (row < col).astype(F32).astype(BF16)
        carry = jnp.zeros((SLABS, 1), F32)
        moment = jnp.zeros((SLABS, COLS), F32)
        for index in range(OBS // chunk):
            part = pl.ds(index * chunk, chunk)
            target = target_ref[:, part]
            place = owner_of(target >> 1) * 2 + (target & 1)
            member = (lax.broadcasted_iota(I32, (SLABS, chunk), 0) == place).astype(F32)
            earlier = jnp.dot(member.astype(BF16), before, preferred_element_type=F32) + carry
            rank = jnp.sum(member * earlier, axis=0, keepdims=True).astype(I32)
            carry = carry + jnp.sum(member, axis=1, keepdims=True)
            slot_ref[:, part] = place * CAP + rank
            weighted = (member * value_ref[:, part]).astype(BF16)
            moment = moment + jnp.dot(weighted, rows_ref[part, :], preferred_element_type=F32)
        moment_ref[...] = moment

    slots = BLOCK_SLABS * CAP
    here = lax.broadcasted_iota(I32, (slots, OBS), 0) + step * slots
    pick = jnp.where(here == slot_ref[...], 1.0, 0.0).astype(BF16)
    sent = jnp.dot(pick, rows_ref[...], preferred_element_type=F32).astype(BF16)
    send_ref[...] = sent.reshape(BLOCK_SLABS, CAP, COLS)


def dispatch(target, value, rows):
    whole = lambda i: (0, 0)
    return pl.pallas_call(
        dispatch_kernel,
        grid=(SLABS // BLOCK_SLABS,),
        in_specs=[
            pl.BlockSpec((1, OBS), whole),
            pl.BlockSpec((1, OBS), whole),
            pl.BlockSpec((OBS, COLS), whole),
        ],
        out_specs=[
            pl.BlockSpec((BLOCK_SLABS, CAP, COLS), lambda i: (i, 0, 0)),
            pl.BlockSpec((SLABS, COLS), whole),
        ],
        out_shape=[
            jax.ShapeDtypeStruct((SLABS, CAP, COLS), BF16),
            jax.ShapeDtypeStruct((SLABS, COLS), F32),
        ],
        scratch_shapes=[pltpu.VMEM((1, OBS), I32)],
        cost_estimate=pl.CostEstimate(
            flops=2 * SLABS * CAP * OBS * COLS, bytes_accessed=10 * 2**20, transcendentals=0
        ),
        compiler_params=pltpu.CompilerParams(vmem_limit_bytes=48 * 2**20),
    )(target, value, rows)


def split(value):
    high = value.astype(BF16)
    return high, (value - high.astype(F32)).astype(BF16)


def product(left, right_high, right_low):
    rows = left.shape[0]
    high, low = split(left)
    both = jnp.dot(jnp.concatenate([high, low]), right_high, preferred_element_type=F32)
    return both[:rows] + (both[rows:] + jnp.dot(high, right_low, preferred_element_type=F32))


def map_kernel(rows_ref, evolve_ref, map_ref, info_ref, high_ref, low_ref):
    step = pl.program_id(0)

    @pl.when(step == 0)
    def _():
        info_ref[...] = jnp.zeros_like(info_ref)

    left = rows_ref[:, 0].reshape(INFO_ROWS, COLS)
    right = rows_ref[:, 1].reshape(INFO_ROWS, COLS)

    def gram(a, b):
        return lax.dot_general(a, b, (((0,), (0,)), ((), ())), preferred_element_type=F32)

    info_ref[:COLS, :COLS] += gram(left, left)
    info_ref[:COLS, COLS:] += gram(left, right)
    info_ref[COLS:, COLS:] += gram(right, right)

    @pl.when(step == pl.num_programs(0) - 1)
    def _():
        info_ref[COLS:, :COLS] = info_ref[:COLS, COLS:].T
        high_ref[...], low_ref[...] = split(info_ref[...])
        for index in range(STATE // CHUNK):
            part = pl.ds(index * CHUNK, CHUNK)
            evolve = evolve_ref[part, :]
            map_ref[part, :] = evolve - GAIN * product(evolve, high_ref[...], low_ref[...])


def slab_map(rows, evolve_t):
    shards = INFO_ROWS // CAP
    whole = pl.BlockSpec((STATE, STATE), lambda i: (0, 0))
    return pl.pallas_call(
        map_kernel,
        grid=(TIME_DEVS // shards,),
        in_specs=[pl.BlockSpec((shards, 2, CAP, COLS), lambda i: (i, 0, 0, 0)), whole],
        out_specs=whole,
        out_shape=jax.ShapeDtypeStruct((STATE, STATE), F32),
        scratch_shapes=[
            pltpu.VMEM((STATE, STATE), F32),
            pltpu.VMEM((STATE, STATE), BF16),
            pltpu.VMEM((STATE, STATE), BF16),
        ],
        cost_estimate=pl.CostEstimate(
            flops=2 * STATE * STATE * (TIME_DEVS * CAP + 3 * STATE),
            bytes_accessed=16 * 2**20,
            transcendentals=0,
        ),
        compiler_params=pltpu.CompilerParams(vmem_limit_bytes=48 * 2**20),
    )(rows, evolve_t)


def pair_kernel(core_ref, own_ref, other_ref, offsets_ref, high_ref, low_ref, half_ref, offset_ref, first_half_ref, h_ref, l_ref):
    def run(first_ref, last_ref, start):
        h_ref[...], l_ref[...] = split(last_ref[...])
        for index in range(0, STATE, CHUNK):
            part = pl.ds(index, CHUNK)
            made = product(first_ref[part, :], h_ref[...], l_ref[...])
            high_ref[part, :], low_ref[part, :] = split(made)
            if start <= index < start + COLS:
                half_ref[pl.ds(index - start, CHUNK), :] = made
        first_half_ref[...] = first_ref[:, start : start + COLS]
        first = jnp.broadcast_to(offsets_ref[0:1, :], (16, STATE))
        offset_ref[...] = product(first, h_ref[...], l_ref[...])[0:1] + offsets_ref[1:2, :]

    @pl.when(core_ref[0] == 0)
    def _():
        run(own_ref, other_ref, 0)

    @pl.when(core_ref[0] == 1)
    def _():
        run(other_ref, own_ref, COLS)


VMEM = pl.BlockSpec(memory_space=pltpu.VMEM)
SMEM = pl.BlockSpec(memory_space=pltpu.SMEM)


def shape(rows, dtype):
    return jax.ShapeDtypeStruct((rows, STATE), dtype)


def pair_map(core, own_t, other_t, offsets):
    return pl.pallas_call(
        pair_kernel,
        in_specs=[SMEM, VMEM, VMEM, VMEM],
        out_specs=[VMEM] * 5,
        out_shape=[
            shape(STATE, BF16),
            shape(STATE, BF16),
            shape(COLS, F32),
            shape(1, F32),
            jax.ShapeDtypeStruct((STATE, COLS), F32),
        ],
        scratch_shapes=[pltpu.VMEM((STATE, STATE), BF16)] * 2,
        cost_estimate=pl.CostEstimate(
            flops=6 * STATE**3, bytes_accessed=16 * 2**20, transcendentals=0
        ),
        compiler_params=pltpu.CompilerParams(vmem_limit_bytes=48 * 2**20),
    )(core, own_t, other_t, offsets)


def step_kernel(step, turn_ref, arrived_ref, opening_ref, offset_ref, high_ref, low_ref, out_ref):
    turn = turn_ref[0]
    made = product(arrived_ref[...], high_ref[...], low_ref[...])
    out_ref[...] = jnp.where(turn == 0, opening_ref[...], made)

    @pl.when((turn > 0) & (step - LAG * turn == BLOCKS))
    def _():
        out_ref[0:1, :] += offset_ref[...]


def advance(step, turn, arrived, opening, offset, high, low):
    return pl.pallas_call(
        functools.partial(step_kernel, step),
        in_specs=[SMEM] + [VMEM] * 5,
        out_specs=VMEM,
        out_shape=jax.ShapeDtypeStruct(arrived.shape, F32),
        cost_estimate=pl.CostEstimate(
            flops=6 * arrived.shape[0] * STATE**2, bytes_accessed=4 * 2**20, transcendentals=0
        ),
        compiler_params=pltpu.CompilerParams(vmem_limit_bytes=24 * 2**20),
    )(turn, arrived, opening, offset, high, low)


def select_kernel(turn_ref, *refs):
    made_refs, (half_ref, shift_ref) = refs[:-2], refs[-2:]
    width = COLS // BLOCKS
    for turn in range(GROUP):

        @pl.when(turn_ref[0] == turn)
        def _(mine=made_refs[LAG * turn :]):
            for index in range(BLOCKS):
                half_ref[pl.ds(index * width, width), :] = mine[index][...]
            shift_ref[...] = mine[BLOCKS][0:1, :]


def select(turn, made):
    return pl.pallas_call(
        select_kernel,
        in_specs=[SMEM] + [VMEM] * len(made),
        out_specs=[VMEM] * 2,
        out_shape=[shape(COLS, F32), shape(1, F32)],
        compiler_params=pltpu.CompilerParams(vmem_limit_bytes=24 * 2**20),
    )(turn, *made)


def gather_kernel(core_ref, own_ref, other_ref, whole_ref):
    @pl.when(core_ref[0] == 0)
    def _():
        whole_ref[:COLS, :] = own_ref[...]
        whole_ref[COLS:, :] = other_ref[...]

    @pl.when(core_ref[0] == 1)
    def _():
        whole_ref[:COLS, :] = other_ref[...]
        whole_ref[COLS:, :] = own_ref[...]


def gather(core, own, other):
    return pl.pallas_call(
        gather_kernel,
        in_specs=[SMEM, VMEM, VMEM],
        out_specs=VMEM,
        out_shape=shape(STATE, F32),
        compiler_params=pltpu.CompilerParams(vmem_limit_bytes=24 * 2**20),
    )(core, own, other)


def apply(matrix_t, vector):
    return jnp.sum(matrix_t * vector[:, None], axis=0)


def along_line(value, steps, closed=True):
    pairs = [
        (i, i // GROUP * GROUP + (i + steps) % GROUP)
        for i in range(TIME_DEVS)
        if closed or i % GROUP + steps < GROUP
    ]
    return lax.ppermute(value, "tm", pairs)


def share_over(value, stride):
    place = lax.axis_index("tm") // stride % 4
    parts = value.reshape(4, -1, *value.shape[1:])
    total = lax.dynamic_index_in_dim(parts, place, keepdims=False)
    for steps in (1, 2, 3):
        pairs = [
            (i, i // (4 * stride) * (4 * stride) + (i + steps * stride) % (4 * stride))
            for i in range(TIME_DEVS)
        ]
        sent = lax.dynamic_index_in_dim(parts, (place + steps) % 4, keepdims=False)
        total = total + lax.ppermute(sent, "tm", pairs)
    return total


def body(initial, dynamics, obs_rows, obs_values, obs_slab):
    position = owner_of(lax.axis_index("tm"))
    second = lax.axis_index("row") == 1
    swap = [(0, 1), (1, 0)]
    send, partial = dispatch(
        obs_slab.reshape(1, OBS), obs_values.astype(F32).reshape(1, OBS), obs_rows
    )
    received = lax.all_to_all(send, ("tm", "row"), split_axis=0, concat_axis=0, tiled=True)
    evolve_t = jnp.eye(STATE, dtype=F32) + dynamics.T
    moment = share_over(partial.reshape(TIME_DEVS, 2, COLS), 16)
    received, moment, evolve_t = lax.optimization_barrier((received, moment, evolve_t))
    own_t = slab_map(received.reshape(TIME_DEVS, 2, CAP, COLS), evolve_t)
    planes = [list(range(start, start + 16)) for start in range(0, TIME_DEVS, 16)]
    moment = lax.all_to_all(
        moment.reshape(16, 2 * COLS), "tm", 0, 0, tiled=True, axis_index_groups=planes
    )
    own_t, moment = lax.optimization_barrier((own_t, moment))
    other_t = lax.ppermute(own_t, "row", swap)
    mine = GAIN * jnp.sum(moment, axis=0).reshape(2, COLS)
    theirs = lax.ppermute(mine, "row", swap)
    offsets = jnp.where(
        second,
        jnp.concatenate([theirs, mine], axis=1),
        jnp.concatenate([mine, theirs], axis=1),
    )
    core = lax.axis_index("row").astype(I32).reshape(1)
    high, low, own_half, offset, first_half_t = pair_map(core, own_t, other_t, offsets)

    turn = position % GROUP
    leads = turn == 0
    turn_scalar = turn.astype(I32).reshape(1)
    width = COLS // BLOCKS
    opening = [own_half[index * width :][:width] for index in range(BLOCKS)]
    opening.append(jnp.pad(offset, ((0, width - 1), (0, 0))))
    made = []
    for step in range(BLOCKS + 1 + LAG * (GROUP - 1)):
        block = opening[min(step, BLOCKS)]
        if step >= LAG:
            arrived = along_line(made[step - LAG], 1, CLOSED)
            block = advance(step, turn_scalar, arrived, block, offset, high, low)
        made.append(block)
    own, shift = select(turn_scalar, made)
    prefix_t = gather(core, own, lax.ppermute(own, "row", swap))

    def whole_prefix(takes, arrived, held):
        entry = jnp.where(takes, arrived, held)
        return entry, apply(prefix_t, entry) + shift[0]

    entry = initial
    entry, after = whole_prefix(leads, entry, entry)
    later = position >= GROUP
    next_line = [(owner_of(t), owner_of((t + GROUP) % TIME_DEVS)) for t in range(TIME_DEVS)]
    for _ in range(TIME_DEVS // GROUP - 1):
        arrived = lax.ppermute(after, "tm", next_line)
        entry, after = whole_prefix(later, arrived, entry)
    held = entry
    for steps in range(1, GROUP):
        entry = jnp.where(turn == steps - 1, along_line(held, steps), entry)
    entry, after = whole_prefix(leads, entry, entry)
    before = jnp.where(leads, entry, along_line(after, 1))
    middle = apply(first_half_t, before) + mine[0]
    after = jnp.where(second, after[COLS:], after[:COLS])
    states = jnp.stack([middle, after])
    return lax.ppermute(states, "tm", [(owner_of(t), t) for t in range(TIME_DEVS)])


def solution(mesh):
    placed = (P(), P(), P("tm", "row"), P("tm"), P("tm", None))
    return jax.shard_map(
        body, mesh=mesh, in_specs=placed, out_specs=P("tm", "row"), check_vma=False
    )
```

```python
import functools

import jax
import jax.numpy as jnp
from jax import lax
from jax.experimental import pallas as pl
from jax.experimental.pallas import tpu as pltpu
from jax.sharding import PartitionSpec as P

F32 = jnp.float32
BF16 = jnp.bfloat16
I32 = jnp.int32
OBS = 2048
CAP = 64
COLS = 512
STATE = 1024
SLABS = 128
TIME_DEVS = 64
BLOCK_SLABS = 8
WINDOW = 640
INFO_ROWS = 1024
GAIN = 0.3
GROUP = 4
BLOCKS = 16
LAG = 3
CHUNK = 256
CLOSED = True


def owner_of(position):
    return position ^ (((position >> 4) & 1) * 12)


def dispatch_kernel(target_ref, value_ref, rows_ref, send_ref, moment_ref, sorted_ref, start_ref):
    step = pl.program_id(0)

    @pl.when(step == 0)
    def _():
        chunk = 256
        row = lax.broadcasted_iota(I32, (chunk, chunk), 0)
        col = lax.broadcasted_iota(I32, (chunk, chunk), 1)
        before = (row < col).astype(F32).astype(BF16)
        target = target_ref[...]
        place = owner_of(target >> 1) * 2 + (target & 1)
        member = (lax.broadcasted_iota(I32, (SLABS, OBS), 0) == place).astype(F32)
        count = jnp.broadcast_to(jnp.sum(member, axis=1, keepdims=True), (SLABS, SLABS))
        row = lax.broadcasted_iota(I32, (SLABS, SLABS), 0)
        col = lax.broadcasted_iota(I32, (SLABS, SLABS), 1)
        above = (col < row).astype(F32).astype(BF16)
        start = jnp.dot(above, count.astype(BF16), preferred_element_type=F32)
        start_ref[...] = start.astype(I32)
        carry = start[:, 0:1]
        moment = jnp.zeros((SLABS, COLS), F32)
        found = []
        for index in range(OBS // chunk):
            part = slice(index * chunk, (index + 1) * chunk)
            ours = member[:, part]
            earlier = jnp.dot(ours.astype(BF16), before, preferred_element_type=F32) + carry
            found.append(jnp.sum(ours * earlier, axis=0, keepdims=True).astype(I32))
            carry = carry + jnp.sum(ours, axis=1, keepdims=True)
            weighted = (ours * value_ref[:, part]).astype(BF16)
            moment = moment + jnp.dot(weighted, rows_ref[part, :], preferred_element_type=F32)
        moment_ref[...] = moment
        found = jnp.concatenate(found, axis=1)
        for index in range(0, OBS, 512):
            here = lax.broadcasted_iota(I32, (512, OBS), 0) + index
            pick = jnp.where(here == found, 1.0, 0.0).astype(BF16)
            ranked = jnp.dot(pick, rows_ref[...], preferred_element_type=F32).astype(BF16)
            sorted_ref[pl.ds(index, 512), :] = ranked
        sorted_ref[OBS:, :] = jnp.zeros((WINDOW, COLS), BF16)

    slots = BLOCK_SLABS * CAP
    start = start_ref[...]
    first = lax.broadcasted_iota(I32, (SLABS, SLABS), 0) == step * BLOCK_SLABS
    begin = jnp.max(jnp.where(first, start, 0))
    begin = pl.multiple_of(begin // 16 * 16, 16)
    at = lax.broadcasted_iota(I32, (1, WINDOW), 1) + begin
    opened = start[:, 0:1] <= at
    place = jnp.sum(opened.astype(I32), axis=0, keepdims=True) - 1
    rank = at - jnp.max(jnp.where(opened, start[:, 0:1], 0), axis=0, keepdims=True)
    slot = jnp.where(at < OBS, (place - step * BLOCK_SLABS) * CAP + rank, -1)
    here = lax.broadcasted_iota(I32, (slots, WINDOW), 0)
    pick = jnp.where(here == slot, 1.0, 0.0).astype(BF16)
    window = sorted_ref[pl.ds(begin, WINDOW), :]
    sent = jnp.dot(pick, window, preferred_element_type=F32).astype(BF16)
    send_ref[...] = sent.reshape(BLOCK_SLABS, CAP, COLS)


def dispatch(target, value, rows):
    whole = lambda i: (0, 0)
    return pl.pallas_call(
        dispatch_kernel,
        grid=(SLABS // BLOCK_SLABS,),
        in_specs=[
            pl.BlockSpec((1, OBS), whole),
            pl.BlockSpec((1, OBS), whole),
            pl.BlockSpec((OBS, COLS), whole),
        ],
        out_specs=[
            pl.BlockSpec((BLOCK_SLABS, CAP, COLS), lambda i: (i, 0, 0)),
            pl.BlockSpec((SLABS, COLS), whole),
        ],
        out_shape=[
            jax.ShapeDtypeStruct((SLABS, CAP, COLS), BF16),
            jax.ShapeDtypeStruct((SLABS, COLS), F32),
        ],
        scratch_shapes=[pltpu.VMEM((OBS + WINDOW, COLS), BF16), pltpu.VMEM((SLABS, SLABS), I32)],
        cost_estimate=pl.CostEstimate(
            flops=2 * SLABS * CAP * OBS * COLS, bytes_accessed=10 * 2**20, transcendentals=0
        ),
        compiler_params=pltpu.CompilerParams(vmem_limit_bytes=48 * 2**20),
    )(target, value, rows)


def split(value):
    high = value.astype(BF16)
    return high, (value - high.astype(F32)).astype(BF16)


def product(left, right_high, right_low):
    rows = left.shape[0]
    high, low = split(left)
    both = jnp.dot(jnp.concatenate([high, low]), right_high, preferred_element_type=F32)
    return both[:rows] + (both[rows:] + jnp.dot(high, right_low, preferred_element_type=F32))


def map_kernel(rows_ref, evolve_ref, map_ref, info_ref, high_ref, low_ref):
    step = pl.program_id(0)

    @pl.when(step == 0)
    def _():
        info_ref[...] = jnp.zeros_like(info_ref)

    left = rows_ref[:, 0].reshape(INFO_ROWS, COLS)
    right = rows_ref[:, 1].reshape(INFO_ROWS, COLS)

    def gram(a, b):
        return lax.dot_general(a, b, (((0,), (0,)), ((), ())), preferred_element_type=F32)

    info_ref[:COLS, :COLS] += gram(left, left)
    info_ref[:COLS, COLS:] += gram(left, right)
    info_ref[COLS:, COLS:] += gram(right, right)

    @pl.when(step == pl.num_programs(0) - 1)
    def _():
        info_ref[COLS:, :COLS] = info_ref[:COLS, COLS:].T
        high_ref[...], low_ref[...] = split(info_ref[...])
        for index in range(STATE // CHUNK):
            part = pl.ds(index * CHUNK, CHUNK)
            evolve = evolve_ref[part, :]
            map_ref[part, :] = evolve - GAIN * product(evolve, high_ref[...], low_ref[...])


def slab_map(rows, evolve_t):
    shards = INFO_ROWS // CAP
    whole = pl.BlockSpec((STATE, STATE), lambda i: (0, 0))
    return pl.pallas_call(
        map_kernel,
        grid=(TIME_DEVS // shards,),
        in_specs=[pl.BlockSpec((shards, 2, CAP, COLS), lambda i: (i, 0, 0, 0)), whole],
        out_specs=whole,
        out_shape=jax.ShapeDtypeStruct((STATE, STATE), F32),
        scratch_shapes=[
            pltpu.VMEM((STATE, STATE), F32),
            pltpu.VMEM((STATE, STATE), BF16),
            pltpu.VMEM((STATE, STATE), BF16),
        ],
        cost_estimate=pl.CostEstimate(
            flops=2 * STATE * STATE * (TIME_DEVS * CAP + 3 * STATE),
            bytes_accessed=16 * 2**20,
            transcendentals=0,
        ),
        compiler_params=pltpu.CompilerParams(vmem_limit_bytes=48 * 2**20),
    )(rows, evolve_t)


def pair_kernel(core_ref, own_ref, other_ref, offsets_ref, high_ref, low_ref, half_ref, offset_ref, first_half_ref, h_ref, l_ref):
    def run(first_ref, last_ref, start):
        h_ref[...], l_ref[...] = split(last_ref[...])
        for index in range(0, STATE, CHUNK):
            part = pl.ds(index, CHUNK)
            made = product(first_ref[part, :], h_ref[...], l_ref[...])
            high_ref[part, :], low_ref[part, :] = split(made)
            if start <= index < start + COLS:
                half_ref[pl.ds(index - start, CHUNK), :] = made
        first_half_ref[...] = first_ref[:, start : start + COLS]
        first = jnp.broadcast_to(offsets_ref[0:1, :], (16, STATE))
        offset_ref[...] = product(first, h_ref[...], l_ref[...])[0:1] + offsets_ref[1:2, :]

    @pl.when(core_ref[0] == 0)
    def _():
        run(own_ref, other_ref, 0)

    @pl.when(core_ref[0] == 1)
    def _():
        run(other_ref, own_ref, COLS)


VMEM = pl.BlockSpec(memory_space=pltpu.VMEM)
SMEM = pl.BlockSpec(memory_space=pltpu.SMEM)


def shape(rows, dtype):
    return jax.ShapeDtypeStruct((rows, STATE), dtype)


def pair_map(core, own_t, other_t, offsets):
    return pl.pallas_call(
        pair_kernel,
        in_specs=[SMEM, VMEM, VMEM, VMEM],
        out_specs=[VMEM] * 5,
        out_shape=[
            shape(STATE, BF16),
            shape(STATE, BF16),
            shape(COLS, F32),
            shape(1, F32),
            jax.ShapeDtypeStruct((STATE, COLS), F32),
        ],
        scratch_shapes=[pltpu.VMEM((STATE, STATE), BF16)] * 2,
        cost_estimate=pl.CostEstimate(
            flops=6 * STATE**3, bytes_accessed=16 * 2**20, transcendentals=0
        ),
        compiler_params=pltpu.CompilerParams(vmem_limit_bytes=48 * 2**20),
    )(core, own_t, other_t, offsets)


def step_kernel(step, turn_ref, arrived_ref, opening_ref, offset_ref, high_ref, low_ref, out_ref):
    turn = turn_ref[0]
    made = product(arrived_ref[...], high_ref[...], low_ref[...])
    out_ref[...] = jnp.where(turn == 0, opening_ref[...], made)

    @pl.when((turn > 0) & (step - LAG * turn == BLOCKS))
    def _():
        out_ref[0:1, :] += offset_ref[...]


def advance(step, turn, arrived, opening, offset, high, low):
    return pl.pallas_call(
        functools.partial(step_kernel, step),
        in_specs=[SMEM] + [VMEM] * 5,
        out_specs=VMEM,
        out_shape=jax.ShapeDtypeStruct(arrived.shape, F32),
        cost_estimate=pl.CostEstimate(
            flops=6 * arrived.shape[0] * STATE**2, bytes_accessed=4 * 2**20, transcendentals=0
        ),
        compiler_params=pltpu.CompilerParams(vmem_limit_bytes=24 * 2**20),
    )(turn, arrived, opening, offset, high, low)


def select_kernel(turn_ref, *refs):
    made_refs, (half_ref, shift_ref) = refs[:-2], refs[-2:]
    width = COLS // BLOCKS
    for turn in range(GROUP):

        @pl.when(turn_ref[0] == turn)
        def _(mine=made_refs[LAG * turn :]):
            for index in range(BLOCKS):
                half_ref[pl.ds(index * width, width), :] = mine[index][...]
            shift_ref[...] = mine[BLOCKS][0:1, :]


def select(turn, made):
    return pl.pallas_call(
        select_kernel,
        in_specs=[SMEM] + [VMEM] * len(made),
        out_specs=[VMEM] * 2,
        out_shape=[shape(COLS, F32), shape(1, F32)],
        compiler_params=pltpu.CompilerParams(vmem_limit_bytes=24 * 2**20),
    )(turn, *made)


def gather_kernel(core_ref, own_ref, other_ref, whole_ref):
    @pl.when(core_ref[0] == 0)
    def _():
        whole_ref[:COLS, :] = own_ref[...]
        whole_ref[COLS:, :] = other_ref[...]

    @pl.when(core_ref[0] == 1)
    def _():
        whole_ref[:COLS, :] = other_ref[...]
        whole_ref[COLS:, :] = own_ref[...]


def gather(core, own, other):
    return pl.pallas_call(
        gather_kernel,
        in_specs=[SMEM, VMEM, VMEM],
        out_specs=VMEM,
        out_shape=shape(STATE, F32),
        compiler_params=pltpu.CompilerParams(vmem_limit_bytes=24 * 2**20),
    )(core, own, other)


def apply(matrix_t, vector):
    return jnp.sum(matrix_t * vector[:, None], axis=0)


def along_line(value, steps, closed=True):
    pairs = [
        (i, i // GROUP * GROUP + (i + steps) % GROUP)
        for i in range(TIME_DEVS)
        if closed or i % GROUP + steps < GROUP
    ]
    return lax.ppermute(value, "tm", pairs)


def share_over(value, stride):
    place = lax.axis_index("tm") // stride % 4
    parts = value.reshape(4, -1, *value.shape[1:])
    total = lax.dynamic_index_in_dim(parts, place, keepdims=False)
    for steps in (1, 2, 3):
        pairs = [
            (i, i // (4 * stride) * (4 * stride) + (i + steps * stride) % (4 * stride))
            for i in range(TIME_DEVS)
        ]
        sent = lax.dynamic_index_in_dim(parts, (place + steps) % 4, keepdims=False)
        total = total + lax.ppermute(sent, "tm", pairs)
    return total


def body(initial, dynamics, obs_rows, obs_values, obs_slab):
    position = owner_of(lax.axis_index("tm"))
    second = lax.axis_index("row") == 1
    swap = [(0, 1), (1, 0)]
    send, partial = dispatch(
        obs_slab.reshape(1, OBS), obs_values.astype(F32).reshape(1, OBS), obs_rows
    )
    received = lax.all_to_all(send, ("tm", "row"), split_axis=0, concat_axis=0, tiled=True)
    evolve_t = jnp.eye(STATE, dtype=F32) + dynamics.T
    moment = share_over(partial.reshape(TIME_DEVS, 2, COLS), 16)
    received, moment, evolve_t = lax.optimization_barrier((received, moment, evolve_t))
    own_t = slab_map(received.reshape(TIME_DEVS, 2, CAP, COLS), evolve_t)
    planes = [list(range(start, start + 16)) for start in range(0, TIME_DEVS, 16)]
    moment = lax.all_to_all(
        moment.reshape(16, 2 * COLS), "tm", 0, 0, tiled=True, axis_index_groups=planes
    )
    own_t, moment = lax.optimization_barrier((own_t, moment))
    other_t = lax.ppermute(own_t, "row", swap)
    mine = GAIN * jnp.sum(moment, axis=0).reshape(2, COLS)
    theirs = lax.ppermute(mine, "row", swap)
    offsets = jnp.where(
        second,
        jnp.concatenate([theirs, mine], axis=1),
        jnp.concatenate([mine, theirs], axis=1),
    )
    core = lax.axis_index("row").astype(I32).reshape(1)
    high, low, own_half, offset, first_half_t = pair_map(core, own_t, other_t, offsets)

    turn = position % GROUP
    leads = turn == 0
    turn_scalar = turn.astype(I32).reshape(1)
    width = COLS // BLOCKS
    opening = [own_half[index * width :][:width] for index in range(BLOCKS)]
    opening.append(jnp.pad(offset, ((0, width - 1), (0, 0))))
    made = []
    for step in range(BLOCKS + 1 + LAG * (GROUP - 1)):
        block = opening[min(step, BLOCKS)]
        if step >= LAG:
            arrived = along_line(made[step - LAG], 1, CLOSED)
            block = advance(step, turn_scalar, arrived, block, offset, high, low)
        made.append(block)
    own, shift = select(turn_scalar, made)
    prefix_t = gather(core, own, lax.ppermute(own, "row", swap))

    def whole_prefix(takes, arrived, held):
        entry = jnp.where(takes, arrived, held)
        return entry, apply(prefix_t, entry) + shift[0]

    entry = initial
    entry, after = whole_prefix(leads, entry, entry)
    later = position >= GROUP
    next_line = [(owner_of(t), owner_of((t + GROUP) % TIME_DEVS)) for t in range(TIME_DEVS)]
    for _ in range(TIME_DEVS // GROUP - 1):
        arrived = lax.ppermute(after, "tm", next_line)
        entry, after = whole_prefix(later, arrived, entry)
    held = entry
    for steps in range(1, GROUP):
        entry = jnp.where(turn == steps - 1, along_line(held, steps), entry)
    entry, after = whole_prefix(leads, entry, entry)
    before = jnp.where(leads, entry, along_line(after, 1))
    middle = apply(first_half_t, before) + mine[0]
    after = jnp.where(second, after[COLS:], after[:COLS])
    states = jnp.stack([middle, after])
    return lax.ppermute(states, "tm", [(owner_of(t), t) for t in range(TIME_DEVS)])


def solution(mesh):
    placed = (P(), P(), P("tm", "row"), P("tm"), P("tm", None))
    return jax.shard_map(
        body, mesh=mesh, in_specs=placed, out_specs=P("tm", "row"), check_vma=False
    )
```
